32 devices in a mesh: area: 8 (over z, y), blk: 4 (over x, core).
Axes of the slice: x: 2, y: 2, z: 4, core: 2. Of those that a mesh axis runs over, the one named last changes fastest.
Arguments:
- activity: float32 [64, 4, 64, 128], P('area', 'blk'), may hold values from -8 to 8
- ext_input: bfloat16 [64, 4, 64, 128], P('area', 'blk'), may hold values from -5 to 5
- weights: bfloat16 [24, 4, 128, 512], P('area', 'blk'), may hold values from -0.25 to 0.25
- slot_dst: int32 [24], P('area'), may hold values from 0 to 7
- slot_src: int32 [24], P('area'), may hold values from 0 to 63, as said below
- slot_count: int32 [8], P('area'), may hold values from 3 to 3, as said below
- hebb_mask: int32 [24], P('area'), may hold values 0 or 1
Outputs:
- final_activity: float32 [64, 4, 64, 128], P('area', 'blk')
- plasticity: bfloat16 [24, 4, 128, 512], P('area', 'blk')
The draws below stay inside these ranges and needn't reach their ends.
Inputs may be any that keep to these rules, and one draw needn't show every extreme that they name: Index i of area holds area i // 4; sources lie in areas listed for it by a connectome over the areas that always lists the area itself, the areas beside it on both sides (counted round) and the opposite one. Slots 0, 1 and 2 of index i of area have their source sub-blocks held by indices (i - 1) mod 8, (i + 1) mod 8 and (i + 4) mod 8. Among the occupied slots of one index of area, at most 1 have source sub-blocks held by one index of area (slot_src // 8); some index of area reaches 1. `slot_count`: some index of area has all 3 slots occupied.
All inputs are finite; a program needn't handle non-finite values. No bound on the sum of `hebb_mask` on one device may be relied on, other than what follows from the above.
Results may differ from the reference program's by a relative error of at most 0.014.
Values may be sent and summed in bfloat16 or wider, within the bound.
A program may use at most 64 MiB of HBM per device.

```python
import jax
import jax.numpy as jnp
from jax import lax

SUB = 512
SPLIT = 4
TRIALS = 64
STEPS = 4
CAP = 3
SUB_DEV = 8
QW = 128
NSUB = 64
SLOTS = 24
N_AREA = 8
N_BLK = 4


def draw_slot_src(key, part):
    n_areas = N_AREA // SPLIT
    listed = jax.random.randint(jax.random.fold_in(key, 13), (n_areas, n_areas), 0, 3) < 2
    forced_span = (CAP + SPLIT - 1) // SPLIT
    gap_areas = (jnp.arange(n_areas)[None, :] - jnp.arange(n_areas)[:, None]) % n_areas
    listed = listed | (gap_areas < forced_span) | (gap_areas == n_areas // 2) | (gap_areas == 1) | (gap_areas == n_areas - 1)
    owner_area = jnp.arange(N_AREA) // SPLIT
    owner_listed = listed[owner_area][:, owner_area].astype(jnp.int32)
    row_keys = jax.random.split(jax.random.fold_in(key, 11), N_AREA)

    def one_order(row_lookup_key):
        return jax.random.permutation(row_lookup_key, N_AREA)
    orders = jax.vmap(one_order)(row_keys).astype(jnp.int32)
    own_index = jnp.arange(N_AREA)
    prev_owner = (own_index + N_AREA - 1) % N_AREA
    next_owner = (own_index + 1) % N_AREA
    far_owner = (own_index + N_AREA // 2) % N_AREA
    is_prev = (own_index[None, :] == prev_owner[:, None]).astype(jnp.int32)
    is_next = (own_index[None, :] == next_owner[:, None]).astype(jnp.int32)
    is_far = (own_index[None, :] == far_owner[:, None]).astype(jnp.int32)
    scores = orders + N_AREA * (1 - owner_listed) - 4 * N_AREA * is_prev - 3 * N_AREA * is_next - 2 * N_AREA * is_far
    sorted_owners = jnp.argsort(scores, axis=1, stable=True).astype(jnp.int32)
    n_listed = jnp.sum(owner_listed, axis=1)
    pick_pos = (jnp.arange(CAP)[None, :] % n_listed[:, None]).astype(jnp.int32)
    owner_idx = jnp.take_along_axis(sorted_owners, pick_pos, axis=1)
    local_idx = jax.random.randint(jax.random.fold_in(key, 12), (N_AREA, CAP), 0, SUB_DEV)
    return (owner_idx * SUB_DEV + local_idx).reshape(N_AREA * CAP).astype(jnp.int32)


def draw_slot_count(key, part):
    first_draw = jax.random.randint(jax.random.fold_in(key, 21), (N_AREA,), 0, CAP)
    second_draw = jax.random.randint(jax.random.fold_in(key, 22), (N_AREA,), 0, CAP)
    counts = jnp.minimum(3 + first_draw * second_draw // CAP, CAP)
    chosen = jax.random.randint(jax.random.fold_in(key, 23), (), 0, N_AREA)
    return jnp.where(jnp.arange(N_AREA) == chosen, CAP, counts).astype(jnp.int32)


def set_ends(values, stream_key, smallest, largest):
    longest = values.shape.index(max(values.shape))
    spots = []
    for shift in (0, 1):
        where = [jax.random.randint(jax.random.fold_in(stream_key, axis), (), 0, length) for axis, length in enumerate(values.shape)]
        where[longest] = (where[longest] + shift) % values.shape[longest]
        spots.append(tuple(where))
    return values.at[spots[0]].set(smallest).at[spots[1]].set(largest)


def block_scale(rng, shape, cuts, low, high):
    def one(axis_at, shards_of):
        heights = jax.random.uniform(jax.random.fold_in(jax.random.fold_in(rng, 6), axis_at), (shards_of,), jnp.float32, low / len(cuts), high / len(cuts))
        return jnp.repeat(jnp.exp(heights), shape[axis_at] // shards_of).reshape((-1,) + (1,) * (len(shape) - axis_at - 1))

    level = one(*cuts[0])
    for cut in cuts[1:]:
        level = level * one(*cut)
    return level


def gaussian(own_key, extent, scale, limit, pieces=(), kind=jnp.bfloat16):
    values = jax.random.normal(own_key, extent, jnp.float32) * scale
    if len(pieces) > 0:
        values = block_scale(own_key, extent, pieces, -0.22, 0.18) * values
    return jnp.clip(values, min=-limit, max=limit).astype(kind)


def setup_inputs(seed: int = 0) -> dict:
    arg_keys = jax.random.split(jax.random.key(seed), 8)
    activity = gaussian(arg_keys[0], (NSUB, N_BLK, TRIALS, QW), 1.5, 8.0, ((0, 8), (1, 4)), jnp.float32)
    ext_input = gaussian(arg_keys[1], (NSUB, N_BLK, TRIALS, QW), 0.7, 5.0, ((0, 8), (1, 4)))
    weights = gaussian(arg_keys[2], (SLOTS, N_BLK, QW, SUB), SUB ** -0.5, 0.25, ((0, 8), (1, 4)))
    slot_dst = set_ends(jax.random.randint(arg_keys[3], (SLOTS,), 0, SUB_DEV), jax.random.fold_in(arg_keys[3], 1), 0, SUB_DEV - 1).astype(jnp.int32)
    slot_src = draw_slot_src(jax.random.fold_in(arg_keys[7], 71), 0)
    slot_count = draw_slot_count(jax.random.fold_in(arg_keys[7], 71), 0)
    hebb_mask = set_ends((jax.random.randint(arg_keys[6], (SLOTS,), 0, 4) < 3).astype(jnp.int32), jax.random.fold_in(arg_keys[6], 1), 0, 1)
    return dict(activity=activity, ext_input=ext_input, weights=weights, slot_dst=slot_dst, slot_src=slot_src, slot_count=slot_count, hebb_mask=hebb_mask)


euler_step = 0.5


def reference(activity, ext_input, weights, slot_dst, slot_src, slot_count, hebb_mask):
    n_subs, n_parts, trials, quarter = activity.shape
    sub_width = n_parts * quarter
    occupied = (jnp.arange(CAP)[None, :] < slot_count[:, None])
    src_rows = slot_src.reshape(N_AREA, CAP)
    dst_local = slot_dst.reshape(N_AREA, CAP)
    w_holders = weights.reshape(N_AREA, CAP, n_parts, quarter, sub_width)

    def inputs_of(rate_now):
        def holder_inputs(packed):
            w_slot, src_here, dst_here, occ_here = packed
            presynaptic_rates = rate_now[src_here].astype(jnp.float32)
            input_contribution = jnp.einsum("kjtq,kjqs->kjts", presynaptic_rates, w_slot.astype(jnp.float32), precision=lax.Precision.HIGHEST)
            select = ((dst_here[:, None] == jnp.arange(SUB_DEV)[None, :]) & occ_here[:, None]).astype(jnp.float32)
            partial_value = jnp.einsum("kd,kjts->jdts", select, input_contribution, precision=lax.Precision.HIGHEST)
            partial_value = lax.optimization_barrier(partial_value.astype(jnp.bfloat16)).astype(jnp.float32)
            summed = jnp.sum(partial_value, axis=0)
            return summed.reshape(SUB_DEV, trials, n_parts, quarter).transpose(0, 2, 1, 3)

        result = lax.map(holder_inputs, (w_holders, src_rows, dst_local, occupied))
        return result.reshape(n_subs, n_parts, trials, quarter)

    current = activity
    drive_in = ext_input.astype(jnp.float32)
    rate_now = jnp.tanh(current).astype(jnp.bfloat16)
    rate_list = [rate_now]
    for step_idx in range(STEPS):
        current = current + euler_step * (inputs_of(rate_now) - current + drive_in)
        rate_now = jnp.tanh(current).astype(jnp.bfloat16)
        rate_list.append(rate_now)
    stacked = jnp.stack(rate_list).astype(jnp.float32)
    centered = (stacked - jnp.mean(stacked, axis=3, keepdims=True)).astype(jnp.bfloat16)
    pre_all = centered[:STEPS]
    post_all = centered[1:]
    gates = (occupied & (hebb_mask.reshape(N_AREA, CAP) == 1)).astype(jnp.float32)
    dst_global = (jnp.arange(N_AREA)[:, None] * SUB_DEV + dst_local).astype(jnp.int32)
    norm_scale = (STEPS * trials) ** -0.5

    def holder_update(packed):
        src_here, dst_here, gate_on = packed
        presynaptic_rates = pre_all[:, src_here].astype(jnp.float32)
        postsynaptic_whole = post_all[:, dst_here].transpose(0, 1, 3, 2, 4).reshape(STEPS, CAP, trials, sub_width).astype(jnp.float32)
        change = jnp.einsum("tkjnq,tkns->kjqs", presynaptic_rates, postsynaptic_whole, precision=lax.Precision.HIGHEST)
        return (change * gate_on[:, None, None, None] * norm_scale).astype(jnp.bfloat16)

    plasticity = lax.map(holder_update, (src_rows, dst_global, gates))
    return current, plasticity.reshape(N_AREA * CAP, n_parts, quarter, sub_width)
```

```python
import functools

import jax
import jax.numpy as jnp
from jax import lax
from jax.experimental import pallas as pl
from jax.experimental.pallas import tpu as pltpu
from jax.sharding import PartitionSpec as P

STEPS = 4
EULER = 0.5
MESH = pl.DeviceIdType.MESH


def kernel(
    n_area,
    n_blk,
    dst_ref,
    src_ref,
    count_ref,
    hebb_ref,
    act_ref,
    ext_ref,
    w_ref,
    out_act,
    out_pl,
    act,
    rate_send,
    rate_recv,
    w_full,
    req_send,
    req_recv,
    post,
    pre,
    acc,
    req_ss,
    req_rs,
    w_ss,
    w_rs,
    r_ss,
    r_rs,
    p_ss,
    p_rs,
):
    n_sub, trials, quarter = act_ref.shape
    slots = w_ref.shape[0]
    a = lax.axis_index("area")
    b = lax.axis_index("blk")
    half = n_area // 2
    readers = (lax.rem(a + 1, n_area), lax.rem(a + n_area - 1, n_area), lax.rem(a + half, n_area))
    owners = (lax.rem(a + n_area - 1, n_area), lax.rem(a + 1, n_area), lax.rem(a + half, n_area))
    sibs = [lax.rem(b + s, n_blk) for s in range(1, n_blk)]
    order = (2, 0, 1)

    barrier = pltpu.get_barrier_semaphore()
    for k in range(slots):
        for s in range(n_blk):
            pl.semaphore_signal(
                barrier, inc=1, device_id=(readers[k], lax.rem(b + s, n_blk)), device_id_type=MESH
            )
    for s in sibs:
        pl.semaphore_signal(barrier, inc=1, device_id=(a, s), device_id_type=MESH)
    for k in range(slots):
        req_send[k] = jnp.full(req_send.shape[1:], lax.rem(src_ref[k], n_sub), jnp.int32)
    pl.semaphore_wait(barrier, slots * n_blk + n_blk - 1)

    pending = []
    req = []
    for k in order:
        c = pltpu.make_async_remote_copy(
            src_ref=req_send.at[k],
            dst_ref=req_recv.at[k],
            send_sem=req_ss.at[k],
            recv_sem=req_rs.at[k],
            device_id=(owners[k], b),
            device_id_type=MESH,
        )
        c.start()
        req.append(c)
        pending.append(c)

    def part(index):
        return pl.ds(pl.multiple_of(index * quarter, quarter), quarter)

    w_copies = []
    for n, s in enumerate(sibs):
        c = pltpu.make_async_remote_copy(
            src_ref=w_ref.at[:, :, part(s)],
            dst_ref=w_full.at[:, part(b), :],
            send_sem=w_ss.at[n],
            recv_sem=w_rs.at[n],
            device_id=(a, s),
            device_id_type=MESH,
        )
        c.start()
        w_copies.append(c)
        pending.append(c)

    act[...] = act_ref[...]
    for k in range(slots):
        w_full[k, part(b), :] = w_ref[k, :, part(b)]
    dst = [dst_ref[k] for k in range(slots)]
    occ = [(k < count_ref[0]).astype(jnp.float32) for k in range(slots)]

    for c in req:
        c.wait_recv()
    want = [jnp.max(req_recv[k]) for k in range(slots)]

    def center(x):
        x = x.astype(jnp.float32)
        return (x - jnp.mean(x, axis=0, keepdims=True)).astype(jnp.bfloat16)

    def updated(index, contrib):
        total = ext_ref[index].astype(jnp.float32)
        for k in range(slots):
            gate = (dst[k] == index).astype(jnp.float32) * occ[k]
            total = total + contrib[k] * gate
        now = act[index]
        return now + EULER * (total - now)

    def send_rates(t, rates):
        for k in order:
            rate_send[t, k] = rates[k]
            for s in range(n_blk):
                c = pltpu.make_async_remote_copy(
                    src_ref=rate_send.at[t, k],
                    dst_ref=rate_recv.at[t, k, b],
                    send_sem=r_ss.at[t, k, s],
                    recv_sem=r_rs.at[t, k],
                    device_id=(readers[k], lax.rem(b + s, n_blk)),
                    device_id_type=MESH,
                )
                c.start()
                pending.append(c)

    send_rates(0, [jnp.tanh(act[want[k]]).astype(jnp.bfloat16) for k in range(slots)])
    for c in w_copies:
        c.wait_recv()

    posts = []
    for t in range(STEPS):
        contrib = [None] * slots
        for k in (0, 1, 2):
            pltpu.make_async_copy(rate_recv.at[t, k], rate_recv.at[t, k], r_rs.at[t, k]).wait()
            rates = jnp.concatenate([rate_recv[t, k, j] for j in range(n_blk)], axis=1)
            contrib[k] = jnp.dot(rates, w_full[k], preferred_element_type=jnp.float32)
        if t < STEPS - 1:
            send_rates(
                t + 1,
                [jnp.tanh(updated(want[k], contrib)).astype(jnp.bfloat16) for k in range(slots)],
            )
        for k in range(slots):
            post[t, b, k] = center(jnp.tanh(updated(dst[k], contrib)).astype(jnp.bfloat16))
        step_posts = []
        for n, s in enumerate(sibs):
            c = pltpu.make_async_remote_copy(
                src_ref=post.at[t, b],
                dst_ref=post.at[t, b],
                send_sem=p_ss.at[t, n],
                recv_sem=p_rs.at[t, n],
                device_id=(a, s),
                device_id_type=MESH,
            )
            c.start()
            step_posts.append(c)
            pending.append(c)
        posts.append(step_posts)
        for d in range(n_sub):
            value = updated(d, contrib)
            if t < STEPS - 1:
                act[d] = value
            else:
                out_act[d] = value
        for k in range(slots):
            pre[k, pl.ds(t * trials, trials), :] = center(rate_recv[t, k, b])

    def change(k, first, last):
        x = pre[k, first * trials : last * trials, :]
        y = jnp.concatenate(
            [
                post[first:last, j, k].reshape((last - first) * trials, quarter)
                for j in range(n_blk)
            ],
            axis=1,
        )
        return lax.dot_general(
            x, y, (((0,), (0,)), ((), ())), preferred_element_type=jnp.float32
        )

    for t in range(STEPS - 1):
        for c in posts[t]:
            c.wait_recv()
    for k in range(slots):
        acc[k] = change(k, 0, STEPS - 1)
    for c in posts[STEPS - 1]:
        c.wait_recv()
    scale = (STEPS * trials) ** -0.5
    for k in range(slots):
        gate = occ[k] * (hebb_ref[k] == 1).astype(jnp.float32) * scale
        out_pl[k] = ((acc[k] + change(k, STEPS - 1, STEPS)) * gate).astype(jnp.bfloat16)
    for c in pending:
        c.wait_send()


def body(n_area, n_blk, activity, ext_input, weights, slot_dst, slot_src, slot_count, hebb_mask):
    n_sub, _, trials, quarter = activity.shape
    slots, _, _, width = weights.shape
    vmem = pl.BlockSpec(memory_space=pltpu.VMEM)
    smem = pl.BlockSpec(memory_space=pltpu.SMEM)
    bf16 = jnp.bfloat16
    dma = pltpu.SemaphoreType.DMA
    act, plast = pl.pallas_call(
        functools.partial(kernel, n_area, n_blk),
        out_shape=(
            jax.ShapeDtypeStruct((n_sub, trials, quarter), jnp.float32),
            jax.ShapeDtypeStruct((slots, quarter, width), bf16),
        ),
        in_specs=[smem] * 4 + [vmem] * 3,
        out_specs=(vmem, vmem),
        scratch_shapes=[
            pltpu.VMEM((n_sub, trials, quarter), jnp.float32),
            pltpu.VMEM((STEPS, slots, trials, quarter), bf16),
            pltpu.VMEM((STEPS, slots, n_blk, trials, quarter), bf16),
            pltpu.VMEM((slots, width, quarter), bf16),
            pltpu.VMEM((slots, 8, 128), jnp.int32),
            pltpu.VMEM((slots, 8, 128), jnp.int32),
            pltpu.VMEM((STEPS, n_blk, slots, trials, quarter), bf16),
            pltpu.VMEM((slots, STEPS * trials, quarter), bf16),
            pltpu.VMEM((slots, quarter, width), jnp.float32),
            dma((slots,)),
            dma((slots,)),
            dma((n_blk - 1,)),
            dma((n_blk - 1,)),
            dma((STEPS, slots, n_blk)),
            dma((STEPS, slots)),
            dma((STEPS, n_blk - 1)),
            dma((STEPS, n_blk - 1)),
        ],
        compiler_params=pltpu.CompilerParams(
            collective_id=0, has_side_effects=True, vmem_limit_bytes=24 * 1024 * 1024
        ),
    )(
        slot_dst,
        slot_src,
        slot_count,
        hebb_mask,
        activity.reshape(n_sub, trials, quarter),
        ext_input.reshape(n_sub, trials, quarter),
        weights.reshape(slots, quarter, width),
    )
    return act[:, None], plast[:, None]


def solution(mesh):
    p4 = P("area", "blk", None, None)
    p1 = P("area")
    return jax.shard_map(
        functools.partial(body, mesh.shape["area"], mesh.shape["blk"]),
        mesh=mesh,
        in_specs=(p4, p4, p4, p1, p1, p1, p1),
        out_specs=(p4, p4),
        check_vma=False,
    )
```

```python
import functools

import jax
import jax.numpy as jnp
from jax import lax
from jax.experimental import pallas as pl
from jax.experimental.pallas import tpu as pltpu
from jax.sharding import PartitionSpec as P

STEPS = 4
EULER = 0.5
MESH = pl.DeviceIdType.MESH


def kernel(
    n_area,
    n_blk,
    dst_hbm,
    src_hbm,
    count_hbm,
    hebb_hbm,
    act_hbm,
    ext_hbm,
    w_ref,
    out_act,
    out_pl,
    dst_ref,
    src_ref,
    count_ref,
    hebb_ref,
    act,
    ext_ref,
    rate_send,
    rate_recv,
    w_full,
    req_send,
    req_recv,
    post,
    pre,
    acc,
    req_ss,
    req_rs,
    w_ss,
    w_rs,
    r_ss,
    r_rs,
    p_ss,
    p_rs,
    in_sem,
):
    n_sub, trials, quarter = act.shape
    slots = w_ref.shape[0]
    a = lax.axis_index("area")
    b = lax.axis_index("blk")
    half = n_area // 2
    readers = (lax.rem(a + 1, n_area), lax.rem(a + n_area - 1, n_area), lax.rem(a + half, n_area))
    owners = (lax.rem(a + n_area - 1, n_area), lax.rem(a + 1, n_area), lax.rem(a + half, n_area))
    sibs = [lax.rem(b + s, n_blk) for s in range(1, n_blk)]
    order = (0, 1, 2)

    def part(index):
        return pl.ds(pl.multiple_of(index * quarter, quarter), quarter)

    loads = [
        pltpu.make_async_copy(x, y, in_sem.at[n])
        for n, (x, y) in enumerate(
            (
                (src_hbm, src_ref),
                (dst_hbm, dst_ref),
                (count_hbm, count_ref),
                (hebb_hbm, hebb_ref),
                (act_hbm, act),
                (ext_hbm, ext_ref),
                (w_ref.at[:, :, part(b)], w_full.at[:, part(b), :]),
            )
        )
    ]
    for c in loads:
        c.start()

    barrier = pltpu.get_barrier_semaphore()
    for k in range(slots):
        for s in range(n_blk):
            pl.semaphore_signal(
                barrier, inc=1, device_id=(readers[k], lax.rem(b + s, n_blk)), device_id_type=MESH
            )
    for s in sibs:
        pl.semaphore_signal(barrier, inc=1, device_id=(a, s), device_id_type=MESH)
    loads[0].wait()
    for k in range(slots):
        req_send[k] = jnp.full(req_send.shape[1:], lax.rem(src_ref[k], n_sub), jnp.int32)
    pl.semaphore_wait(barrier, slots * n_blk + n_blk - 1)

    pending = []
    req = []
    for k in order:
        c = pltpu.make_async_remote_copy(
            src_ref=req_send.at[k],
            dst_ref=req_recv.at[k],
            send_sem=req_ss.at[k],
            recv_sem=req_rs.at[k],
            device_id=(owners[k], b),
            device_id_type=MESH,
        )
        c.start()
        req.append(c)
        pending.append(c)

    w_copies = []
    for n, s in enumerate(sibs):
        c = pltpu.make_async_remote_copy(
            src_ref=w_ref.at[:, :, part(s)],
            dst_ref=w_full.at[:, part(b), :],
            send_sem=w_ss.at[n],
            recv_sem=w_rs.at[n],
            device_id=(a, s),
            device_id_type=MESH,
        )
        c.start()
        w_copies.append(c)
        pending.append(c)

    for c in loads[1:]:
        c.wait()
    dst = [dst_ref[k] for k in range(slots)]
    occ = [(k < count_ref[0]).astype(jnp.float32) for k in range(slots)]

    for c in req:
        c.wait_recv()
    want = [jnp.max(req_recv[k]) for k in range(slots)]

    def center(x):
        x = x.astype(jnp.float32)
        return (x - jnp.mean(x, axis=0, keepdims=True)).astype(jnp.bfloat16)

    def updated(index, contrib):
        total = ext_ref[index].astype(jnp.float32)
        for k in range(slots):
            gate = (dst[k] == index).astype(jnp.float32) * occ[k]
            total = total + contrib[k] * gate
        now = act[index]
        return now + EULER * (total - now)

    def send_rates(t, rates):
        for k in order:
            rate_send[t, k] = rates[k]
            for s in range(n_blk):
                c = pltpu.make_async_remote_copy(
                    src_ref=rate_send.at[t, k],
                    dst_ref=rate_recv.at[t, k, b],
                    send_sem=r_ss.at[t, k, s],
                    recv_sem=r_rs.at[t, k],
                    device_id=(readers[k], lax.rem(b + s, n_blk)),
                    device_id_type=MESH,
                )
                c.start()
                pending.append(c)

    send_rates(0, [jnp.tanh(act[want[k]]).astype(jnp.bfloat16) for k in range(slots)])
    for c in w_copies:
        c.wait_recv()

    posts = []
    for t in range(STEPS):
        contrib = [None] * slots
        for k in (0, 1, 2):
            pltpu.make_async_copy(rate_recv.at[t, k], rate_recv.at[t, k], r_rs.at[t, k]).wait()
            rates = jnp.concatenate([rate_recv[t, k, j] for j in range(n_blk)], axis=1)
            contrib[k] = jnp.dot(rates, w_full[k], preferred_element_type=jnp.float32)
        if t < STEPS - 1:
            send_rates(
                t + 1,
                [jnp.tanh(updated(want[k], contrib)).astype(jnp.bfloat16) for k in range(slots)],
            )
        for k in range(slots):
            post[t, b, k] = center(jnp.tanh(updated(dst[k], contrib)).astype(jnp.bfloat16))
        step_posts = []
        for n, s in enumerate(sibs):
            c = pltpu.make_async_remote_copy(
                src_ref=post.at[t, b],
                dst_ref=post.at[t, b],
                send_sem=p_ss.at[t, n],
                recv_sem=p_rs.at[t, n],
                device_id=(a, s),
                device_id_type=MESH,
            )
            c.start()
            step_posts.append(c)
            pending.append(c)
        posts.append(step_posts)
        for d in range(n_sub):
            value = updated(d, contrib)
            if t < STEPS - 1:
                act[d] = value
            else:
                out_act[d] = value
        for k in range(slots):
            pre[k, pl.ds(t * trials, trials), :] = center(rate_recv[t, k, b])

    def change(k, first, last):
        x = pre[k, first * trials : last * trials, :]
        y = jnp.concatenate(
            [
                post[first:last, j, k].reshape((last - first) * trials, quarter)
                for j in range(n_blk)
            ],
            axis=1,
        )
        return lax.dot_general(
            x, y, (((0,), (0,)), ((), ())), preferred_element_type=jnp.float32
        )

    for t in range(STEPS - 1):
        for c in posts[t]:
            c.wait_recv()
    for k in range(slots):
        acc[k] = change(k, 0, STEPS - 1)
    for c in posts[STEPS - 1]:
        c.wait_recv()
    scale = (STEPS * trials) ** -0.5
    for k in range(slots):
        gate = occ[k] * (hebb_ref[k] == 1).astype(jnp.float32) * scale
        out_pl[k] = ((acc[k] + change(k, STEPS - 1, STEPS)) * gate).astype(jnp.bfloat16)
    for c in pending:
        c.wait_send()


def body(n_area, n_blk, activity, ext_input, weights, slot_dst, slot_src, slot_count, hebb_mask):
    n_sub, _, trials, quarter = activity.shape
    slots, _, _, width = weights.shape
    vmem = pl.BlockSpec(memory_space=pltpu.VMEM)
    hbm = pl.BlockSpec(memory_space=pltpu.HBM)
    bf16 = jnp.bfloat16
    dma = pltpu.SemaphoreType.DMA
    act, plast = pl.pallas_call(
        functools.partial(kernel, n_area, n_blk),
        out_shape=(
            jax.ShapeDtypeStruct((n_sub, trials, quarter), jnp.float32),
            jax.ShapeDtypeStruct((slots, quarter, width), bf16),
        ),
        in_specs=[hbm] * 7,
        out_specs=(vmem, vmem),
        scratch_shapes=[
            pltpu.SMEM((slots,), jnp.int32),
            pltpu.SMEM((slots,), jnp.int32),
            pltpu.SMEM((1,), jnp.int32),
            pltpu.SMEM((slots,), jnp.int32),
            pltpu.VMEM((n_sub, trials, quarter), jnp.float32),
            pltpu.VMEM((n_sub, trials, quarter), bf16),
            pltpu.VMEM((STEPS, slots, trials, quarter), bf16),
            pltpu.VMEM((STEPS, slots, n_blk, trials, quarter), bf16),
            pltpu.VMEM((slots, width, quarter), bf16),
            pltpu.VMEM((slots, 8, 128), jnp.int32),
            pltpu.VMEM((slots, 8, 128), jnp.int32),
            pltpu.VMEM((STEPS, n_blk, slots, trials, quarter), bf16),
            pltpu.VMEM((slots, STEPS * trials, quarter), bf16),
            pltpu.VMEM((slots, quarter, width), jnp.float32),
            dma((slots,)),
            dma((slots,)),
            dma((n_blk - 1,)),
            dma((n_blk - 1,)),
            dma((STEPS, slots, n_blk)),
            dma((STEPS, slots)),
            dma((STEPS, n_blk - 1)),
            dma((STEPS, n_blk - 1)),
            dma((7,)),
        ],
        compiler_params=pltpu.CompilerParams(
            collective_id=0, has_side_effects=True, vmem_limit_bytes=24 * 1024 * 1024
        ),
    )(
        slot_dst,
        slot_src,
        slot_count,
        hebb_mask,
        activity.reshape(n_sub, trials, quarter),
        ext_input.reshape(n_sub, trials, quarter),
        weights.reshape(slots, quarter, width),
    )
    return act[:, None], plast[:, None]


def solution(mesh):
    p4 = P("area", "blk", None, None)
    p1 = P("area")
    return jax.shard_map(
        functools.partial(body, mesh.shape["area"], mesh.shape["blk"]),
        mesh=mesh,
        in_specs=(p4, p4, p4, p1, p1, p1, p1),
        out_specs=(p4, p4),
        check_vma=False,
    )
```

```python
import functools

import jax
import jax.numpy as jnp
from jax import lax
from jax.experimental import pallas as pl
from jax.experimental.pallas import tpu as pltpu
from jax.sharding import PartitionSpec as P

STEPS = 4
EULER = 0.5
MESH = pl.DeviceIdType.MESH


def kernel(
    n_area,
    n_blk,
    dst_hbm,
    src_hbm,
    count_hbm,
    hebb_hbm,
    act_hbm,
    ext_hbm,
    w_ref,
    out_act,
    out_pl,
    dst_ref,
    src_ref,
    count_ref,
    hebb_ref,
    act,
    ext_ref,
    rate_send,
    rate_recv,
    w_full,
    req_send,
    req_recv,
    post,
    pre,
    acc,
    req_ss,
    req_rs,
    w_ss,
    w_rs,
    r_ss,
    r_rs,
    p_ss,
    p_rs,
    in_sem,
    plast,
):
    n_sub, trials, quarter = act.shape
    slots = w_ref.shape[0]
    a = lax.axis_index("area")
    b = lax.axis_index("blk")
    half = n_area // 2
    readers = (lax.rem(a + 1, n_area), lax.rem(a + n_area - 1, n_area), lax.rem(a + half, n_area))
    owners = (lax.rem(a + n_area - 1, n_area), lax.rem(a + 1, n_area), lax.rem(a + half, n_area))
    shifts = [n_blk // 2] + [s for s in range(1, n_blk) if s != n_blk // 2]
    sibs = [lax.rem(b + s, n_blk) for s in shifts]
    order = (0, 1, 2)
    sends = [(k, s) for k in order for s in (2, 3, 0, 1)[:n_blk]]

    def part(index):
        return pl.ds(pl.multiple_of(index * quarter, quarter), quarter)

    loads = [
        pltpu.make_async_copy(x, y, in_sem.at[n])
        for n, (x, y) in enumerate(
            (
                (src_hbm, src_ref),
                (dst_hbm, dst_ref),
                (count_hbm, count_ref),
                (hebb_hbm, hebb_ref),
                (act_hbm, act),
                (ext_hbm, ext_ref),
                (w_ref.at[:, :, part(b)], w_full.at[:, part(b), :]),
            )
        )
    ]
    for c in loads:
        c.start()

    barrier = pltpu.get_barrier_semaphore()
    for k in range(slots):
        for s in range(n_blk):
            pl.semaphore_signal(
                barrier, inc=1, device_id=(readers[k], lax.rem(b + s, n_blk)), device_id_type=MESH
            )
    for s in sibs:
        pl.semaphore_signal(barrier, inc=1, device_id=(a, s), device_id_type=MESH)
    loads[0].wait()
    for k in range(slots):
        req_send[k] = jnp.full(req_send.shape[1:], lax.rem(src_ref[k], n_sub), jnp.int32)
    pl.semaphore_wait(barrier, slots * n_blk + n_blk - 1)

    pending = []
    req = []
    for k in order:
        c = pltpu.make_async_remote_copy(
            src_ref=req_send.at[k],
            dst_ref=req_recv.at[k],
            send_sem=req_ss.at[k],
            recv_sem=req_rs.at[k],
            device_id=(owners[k], b),
            device_id_type=MESH,
        )
        c.start()
        req.append(c)
        pending.append(c)

    w_copies = []
    for n, s in enumerate(sibs):
        c = pltpu.make_async_remote_copy(
            src_ref=w_ref.at[:, :, part(s)],
            dst_ref=w_full.at[:, part(b), :],
            send_sem=w_ss.at[n],
            recv_sem=w_rs.at[n],
            device_id=(a, s),
            device_id_type=MESH,
        )
        c.start()
        w_copies.append(c)
        pending.append(c)

    for c in loads[1:]:
        c.wait()
    dst = [dst_ref[k] for k in range(slots)]
    occ = [(k < count_ref[0]).astype(jnp.float32) for k in range(slots)]

    for c in req:
        c.wait_recv()
    want = [jnp.max(req_recv[k]) for k in range(slots)]

    def center(x):
        x = x.astype(jnp.float32)
        return (x - jnp.mean(x, axis=0, keepdims=True)).astype(jnp.bfloat16)

    def updated(index, contrib):
        total = ext_ref[index].astype(jnp.float32)
        for k in range(slots):
            gate = (dst[k] == index).astype(jnp.float32) * occ[k]
            total = total + contrib[k] * gate
        now = act[index]
        return now + EULER * (total - now)

    def send_rates(t, rates):
        for k in order:
            rate_send[t, k] = rates[k]
        for k, s in sends:
            if True:
                c = pltpu.make_async_remote_copy(
                    src_ref=rate_send.at[t, k],
                    dst_ref=rate_recv.at[t, k, b],
                    send_sem=r_ss.at[t, k, s],
                    recv_sem=r_rs.at[t, k],
                    device_id=(readers[k], lax.rem(b + s, n_blk)),
                    device_id_type=MESH,
                )
                c.start()
                pending.append(c)

    send_rates(0, [jnp.tanh(act[want[k]]).astype(jnp.bfloat16) for k in range(slots)])
    for c in w_copies:
        c.wait_recv()

    posts = []
    stores = []
    for t in range(STEPS):
        contrib = [None] * slots
        for k in (0, 1, 2):
            pltpu.make_async_copy(rate_recv.at[t, k], rate_recv.at[t, k], r_rs.at[t, k]).wait()
            rates = jnp.concatenate([rate_recv[t, k, j] for j in range(n_blk)], axis=1)
            contrib[k] = jnp.dot(rates, w_full[k], preferred_element_type=jnp.float32)
        if t < STEPS - 1:
            send_rates(
                t + 1,
                [jnp.tanh(updated(want[k], contrib)).astype(jnp.bfloat16) for k in range(slots)],
            )
        for k in range(slots):
            post[t, b, k] = center(jnp.tanh(updated(dst[k], contrib)).astype(jnp.bfloat16))
        step_posts = []
        for n, s in enumerate(sibs):
            c = pltpu.make_async_remote_copy(
                src_ref=post.at[t, b],
                dst_ref=post.at[t, b],
                send_sem=p_ss.at[t, n],
                recv_sem=p_rs.at[t, n],
                device_id=(a, s),
                device_id_type=MESH,
            )
            c.start()
            step_posts.append(c)
            pending.append(c)
        posts.append(step_posts)
        for d in range(n_sub):
            value = updated(d, contrib)
            act[d] = value
        if t == STEPS - 1:
            stores.append(pltpu.make_async_copy(act, out_act, in_sem.at[0]))
            stores[-1].start()
        for k in range(slots):
            pre[k, pl.ds(t * trials, trials), :] = center(rate_recv[t, k, b])

    def change(k, first, last):
        x = pre[k, first * trials : last * trials, :]
        y = jnp.concatenate(
            [
                post[first:last, j, k].reshape((last - first) * trials, quarter)
                for j in range(n_blk)
            ],
            axis=1,
        )
        return lax.dot_general(
            x, y, (((0,), (0,)), ((), ())), preferred_element_type=jnp.float32
        )

    for t in range(STEPS - 1):
        for c in posts[t]:
            c.wait_recv()
    for k in range(slots):
        acc[k] = change(k, 0, STEPS - 1)
    for c in posts[STEPS - 1]:
        c.wait_recv()
    scale = (STEPS * trials) ** -0.5
    for k in range(slots):
        gate = occ[k] * (hebb_ref[k] == 1).astype(jnp.float32) * scale
        plast[k] = ((acc[k] + change(k, STEPS - 1, STEPS)) * gate).astype(jnp.bfloat16)
        stores.append(pltpu.make_async_copy(plast.at[k], out_pl.at[k], in_sem.at[k + 1]))
        stores[-1].start()
    for c in stores:
        c.wait()
    for c in pending:
        c.wait_send()


def body(n_area, n_blk, activity, ext_input, weights, slot_dst, slot_src, slot_count, hebb_mask):
    n_sub, _, trials, quarter = activity.shape
    slots, _, _, width = weights.shape
    hbm = pl.BlockSpec(memory_space=pl.ANY)
    bf16 = jnp.bfloat16
    dma = pltpu.SemaphoreType.DMA
    act, plast = pl.pallas_call(
        functools.partial(kernel, n_area, n_blk),
        out_shape=(
            jax.ShapeDtypeStruct((n_sub, trials, quarter), jnp.float32),
            jax.ShapeDtypeStruct((slots, quarter, width), bf16),
        ),
        in_specs=[hbm] * 7,
        out_specs=(hbm, hbm),
        scratch_shapes=[
            pltpu.SMEM((slots,), jnp.int32),
            pltpu.SMEM((slots,), jnp.int32),
            pltpu.SMEM((1,), jnp.int32),
            pltpu.SMEM((slots,), jnp.int32),
            pltpu.VMEM((n_sub, trials, quarter), jnp.float32),
            pltpu.VMEM((n_sub, trials, quarter), bf16),
            pltpu.VMEM((STEPS, slots, trials, quarter), bf16),
            pltpu.VMEM((STEPS, slots, n_blk, trials, quarter), bf16),
            pltpu.VMEM((slots, width, quarter), bf16),
            pltpu.VMEM((slots, 8, 128), jnp.int32),
            pltpu.VMEM((slots, 8, 128), jnp.int32),
            pltpu.VMEM((STEPS, n_blk, slots, trials, quarter), bf16),
            pltpu.VMEM((slots, STEPS * trials, quarter), bf16),
            pltpu.VMEM((slots, quarter, width), jnp.float32),
            dma((slots,)),
            dma((slots,)),
            dma((n_blk - 1,)),
            dma((n_blk - 1,)),
            dma((STEPS, slots, n_blk)),
            dma((STEPS, slots)),
            dma((STEPS, n_blk - 1)),
            dma((STEPS, n_blk - 1)),
            dma((7,)),
            pltpu.VMEM((slots, quarter, width), bf16),
        ],
        compiler_params=pltpu.CompilerParams(
            collective_id=0, has_side_effects=True, vmem_limit_bytes=62 * 1024 * 1024
        ),
    )(
        slot_dst,
        slot_src,
        slot_count,
        hebb_mask,
        activity.reshape(n_sub, trials, quarter),
        ext_input.reshape(n_sub, trials, quarter),
        weights.reshape(slots, quarter, width),
    )
    return act[:, None], plast[:, None]


def solution(mesh):
    p4 = P("area", "blk", None, None)
    p1 = P("area")
    return jax.shard_map(
        functools.partial(body, mesh.shape["area"], mesh.shape["blk"]),
        mesh=mesh,
        in_specs=(p4, p4, p4, p1, p1, p1, p1),
        out_specs=(p4, p4),
        check_vma=False,
    )
```

```python
import functools

import jax
import jax.numpy as jnp
from jax import lax
from jax.experimental import pallas as pl
from jax.experimental.pallas import tpu as pltpu
from jax.sharding import PartitionSpec as P

STEPS = 4
EULER = 0.5
MESH = pl.DeviceIdType.MESH


def kernel(
    n_area,
    n_blk,
    dst_hbm,
    src_hbm,
    count_hbm,
    hebb_hbm,
    act_hbm,
    ext_hbm,
    w_ref,
    out_act,
    out_pl,
    dst_ref,
    src_ref,
    count_ref,
    hebb_ref,
    act,
    ext_ref,
    rate_send,
    rate_recv,
    w_full,
    req_send,
    req_recv,
    post,
    pre,
    acc,
    req_ss,
    req_rs,
    w_ss,
    w_rs,
    r_ss,
    r_rs,
    p_ss,
    p_rs,
    in_sem,
    plast,
):
    n_sub, trials, quarter = act.shape
    slots = w_ref.shape[0]
    a = lax.axis_index("area")
    b = lax.axis_index("blk")
    half = n_area // 2
    readers = (lax.rem(a + 1, n_area), lax.rem(a + n_area - 1, n_area), lax.rem(a + half, n_area))
    owners = (lax.rem(a + n_area - 1, n_area), lax.rem(a + 1, n_area), lax.rem(a + half, n_area))
    shifts = [n_blk // 2] + [s for s in range(1, n_blk) if s != n_blk // 2]
    sibs = [lax.rem(b + s, n_blk) for s in shifts]
    order = (0, 1, 2)
    lead = 1 - lax.rem(a, 2)
    near = 1 - lead
    to_lead = lax.rem(a + 1 + lead * (n_area - 2), n_area)
    to_near = lax.rem(a + 1 + near * (n_area - 2), n_area)
    paths = ((lead, to_lead), (near, to_near), (2, readers[2]))
    sends = [(k, to, s) for k, to in paths for s in (2, 3, 0, 1)[:n_blk]]

    def part(index):
        return pl.ds(pl.multiple_of(index * quarter, quarter), quarter)

    loads = [
        pltpu.make_async_copy(x, y, in_sem.at[n])
        for n, (x, y) in enumerate(
            (
                (src_hbm, src_ref),
                (dst_hbm, dst_ref),
                (count_hbm, count_ref),
                (hebb_hbm, hebb_ref),
                (act_hbm, act),
                (ext_hbm, ext_ref),
                (w_ref.at[:, :, part(b)], w_full.at[:, part(b), :]),
            )
        )
    ]
    for c in loads:
        c.start()

    barrier = pltpu.get_barrier_semaphore()
    for k in range(slots):
        for s in range(n_blk):
            pl.semaphore_signal(
                barrier, inc=1, device_id=(readers[k], lax.rem(b + s, n_blk)), device_id_type=MESH
            )
    for s in sibs:
        pl.semaphore_signal(barrier, inc=1, device_id=(a, s), device_id_type=MESH)
    loads[0].wait()
    for k in range(slots):
        req_send[k] = jnp.full(req_send.shape[1:], lax.rem(src_ref[k], n_sub), jnp.int32)
    pl.semaphore_wait(barrier, slots * n_blk + n_blk - 1)

    pending = []
    req = []
    for k in order:
        c = pltpu.make_async_remote_copy(
            src_ref=req_send.at[k],
            dst_ref=req_recv.at[k],
            send_sem=req_ss.at[k],
            recv_sem=req_rs.at[k],
            device_id=(owners[k], b),
            device_id_type=MESH,
        )
        c.start()
        req.append(c)
        pending.append(c)

    w_copies = []
    for n, s in enumerate(sibs):
        c = pltpu.make_async_remote_copy(
            src_ref=w_ref.at[:, :, part(s)],
            dst_ref=w_full.at[:, part(b), :],
            send_sem=w_ss.at[n],
            recv_sem=w_rs.at[n],
            device_id=(a, s),
            device_id_type=MESH,
        )
        c.start()
        w_copies.append(c)
        pending.append(c)

    for c in loads[1:]:
        c.wait()
    dst = [dst_ref[k] for k in range(slots)]
    occ = [(k < count_ref[0]).astype(jnp.float32) for k in range(slots)]

    for c in req:
        c.wait_recv()
    want = [jnp.max(req_recv[k]) for k in range(slots)]

    def center(x):
        x = x.astype(jnp.float32)
        return (x - jnp.mean(x, axis=0, keepdims=True)).astype(jnp.bfloat16)

    def updated(index, contrib):
        total = ext_ref[index].astype(jnp.float32)
        for k in range(slots):
            gate = (dst[k] == index).astype(jnp.float32) * occ[k]
            total = total + contrib[k] * gate
        now = act[index]
        return now + EULER * (total - now)

    def send_rates(t, rates):
        for k in order:
            rate_send[t, k] = rates[k]
        for k, to, s in sends:
            if True:
                c = pltpu.make_async_remote_copy(
                    src_ref=rate_send.at[t, k],
                    dst_ref=rate_recv.at[t, k, b],
                    send_sem=r_ss.at[t, k, s],
                    recv_sem=r_rs.at[t, k],
                    device_id=(to, lax.rem(b + s, n_blk)),
                    device_id_type=MESH,
                )
                c.start()
                pending.append(c)

    send_rates(0, [jnp.tanh(act[want[k]]).astype(jnp.bfloat16) for k in range(slots)])
    for c in w_copies:
        c.wait_recv()

    across = []
    beside = []
    mate = b + 1 - 2 * lax.rem(b, 2)

    def post_copy(t, piece, to, n):
        c = pltpu.make_async_remote_copy(
            src_ref=post.at[t, piece],
            dst_ref=post.at[t, piece],
            send_sem=p_ss.at[t, n],
            recv_sem=p_rs.at[t, n],
            device_id=(a, to),
            device_id_type=MESH,
        )
        c.start()
        pending.append(c)
        return c

    stores = []
    for t in range(STEPS):
        contrib = [None] * slots
        for k in (0, 1, 2):
            pltpu.make_async_copy(rate_recv.at[t, k], rate_recv.at[t, k], r_rs.at[t, k]).wait()
            rates = jnp.concatenate([rate_recv[t, k, j] for j in range(n_blk)], axis=1)
            contrib[k] = jnp.dot(rates, w_full[k], preferred_element_type=jnp.float32)
        if t < STEPS - 1:
            send_rates(
                t + 1,
                [jnp.tanh(updated(want[k], contrib)).astype(jnp.bfloat16) for k in range(slots)],
            )
        for k in range(slots):
            post[t, b, k] = center(jnp.tanh(updated(dst[k], contrib)).astype(jnp.bfloat16))
        if t == STEPS - 1:
            last_posts = [post_copy(t, b, s, n) for n, s in enumerate(sibs)]
        else:
            across.append(post_copy(t, b, sibs[0], 0))
            beside.append(post_copy(t, b, mate, 1))
        if t > 0:
            across[t - 1].wait_recv()
            beside.append(post_copy(t - 1, sibs[0], mate, 2))
        for d in range(n_sub):
            value = updated(d, contrib)
            act[d] = value
        if t == STEPS - 1:
            stores.append(pltpu.make_async_copy(act, out_act, in_sem.at[0]))
            stores[-1].start()
        for k in range(slots):
            pre[k, pl.ds(t * trials, trials), :] = center(rate_recv[t, k, b])

    def change(k, first, last):
        x = pre[k, first * trials : last * trials, :]
        y = jnp.concatenate(
            [
                post[first:last, j, k].reshape((last - first) * trials, quarter)
                for j in range(n_blk)
            ],
            axis=1,
        )
        return lax.dot_general(
            x, y, (((0,), (0,)), ((), ())), preferred_element_type=jnp.float32
        )

    for c in beside:
        c.wait_recv()
    for k in range(slots):
        acc[k] = change(k, 0, STEPS - 1)
    for c in last_posts:
        c.wait_recv()
    scale = (STEPS * trials) ** -0.5
    for k in range(slots):
        gate = occ[k] * (hebb_ref[k] == 1).astype(jnp.float32) * scale
        plast[k] = ((acc[k] + change(k, STEPS - 1, STEPS)) * gate).astype(jnp.bfloat16)
        stores.append(pltpu.make_async_copy(plast.at[k], out_pl.at[k], in_sem.at[k + 1]))
        stores[-1].start()
    for c in stores:
        c.wait()
    for c in pending:
        c.wait_send()


def body(n_area, n_blk, activity, ext_input, weights, slot_dst, slot_src, slot_count, hebb_mask):
    n_sub, _, trials, quarter = activity.shape
    slots, _, _, width = weights.shape
    hbm = pl.BlockSpec(memory_space=pl.ANY)
    bf16 = jnp.bfloat16
    dma = pltpu.SemaphoreType.DMA
    act, plast = pl.pallas_call(
        functools.partial(kernel, n_area, n_blk),
        out_shape=(
            jax.ShapeDtypeStruct((n_sub, trials, quarter), jnp.float32),
            jax.ShapeDtypeStruct((slots, quarter, width), bf16),
        ),
        in_specs=[hbm] * 7,
        out_specs=(hbm, hbm),
        scratch_shapes=[
            pltpu.SMEM((slots,), jnp.int32),
            pltpu.SMEM((slots,), jnp.int32),
            pltpu.SMEM((1,), jnp.int32),
            pltpu.SMEM((slots,), jnp.int32),
            pltpu.VMEM((n_sub, trials, quarter), jnp.float32),
            pltpu.VMEM((n_sub, trials, quarter), bf16),
            pltpu.VMEM((STEPS, slots, trials, quarter), bf16),
            pltpu.VMEM((STEPS, slots, n_blk, trials, quarter), bf16),
            pltpu.VMEM((slots, width, quarter), bf16),
            pltpu.VMEM((slots, 8, 128), jnp.int32),
            pltpu.VMEM((slots, 8, 128), jnp.int32),
            pltpu.VMEM((STEPS, n_blk, slots, trials, quarter), bf16),
            pltpu.VMEM((slots, STEPS * trials, quarter), bf16),
            pltpu.VMEM((slots, quarter, width), jnp.float32),
            dma((slots,)),
            dma((slots,)),
            dma((n_blk - 1,)),
            dma((n_blk - 1,)),
            dma((STEPS, slots, n_blk)),
            dma((STEPS, slots)),
            dma((STEPS, n_blk - 1)),
            dma((STEPS, n_blk - 1)),
            dma((7,)),
            pltpu.VMEM((slots, quarter, width), bf16),
        ],
        compiler_params=pltpu.CompilerParams(
            collective_id=0, has_side_effects=True, vmem_limit_bytes=62 * 1024 * 1024
        ),
    )(
        slot_dst,
        slot_src,
        slot_count,
        hebb_mask,
        activity.reshape(n_sub, trials, quarter),
        ext_input.reshape(n_sub, trials, quarter),
        weights.reshape(slots, quarter, width),
    )
    return act[:, None], plast[:, None]


def solution(mesh):
    p4 = P("area", "blk", None, None)
    p1 = P("area")
    return jax.shard_map(
        functools.partial(body, mesh.shape["area"], mesh.shape["blk"]),
        mesh=mesh,
        in_specs=(p4, p4, p4, p1, p1, p1, p1),
        out_specs=(p4, p4),
        check_vma=False,
    )
```
